32 devices in a mesh: parts: 2 (over x), fsdp: 8 (over z, y), dp: 2 (over core).
Axes of the slice: x: 2, y: 2, z: 4, core: 2. Of those that a mesh axis runs over, the one named last changes fastest.
Arguments:
- tokens: bfloat16 [64, 256, 2048], P(('parts', 'fsdp', 'dp')), parts along dimension 0, may hold values from -6 to 6
- key_shift: bfloat16 [64, 8, 256], P(('parts', 'fsdp', 'dp')), parts along dimension 0, may hold values from -6 to 258
- counts: int32 [64], P('parts'), parts along dimension 0, may hold values from 1 to 32, as said below
- repack_order: int32 [16, 4], P(('parts', 'fsdp')), parts along dimension 0, may hold values from 0 to 3, each once within a row
- norm_gain: float32 [2048], replicated, may hold values from 0.5 to 1.5
- query_weight: bfloat16 [2048, 1024], P('fsdp'), may hold values from -0.125 to 0.125
- key_weight: bfloat16 [2048, 1024], P('fsdp'), may hold values from -0.125 to 0.125
- value_weight: bfloat16 [2048, 1024], P('fsdp'), may hold values from -0.125 to 0.125
- out_weight: bfloat16 [1024, 2048], P('fsdp'), may hold values from -0.1875 to 0.1875
- cotangent: bfloat16 [64, 256, 2048], P(('parts', 'fsdp', 'dp')), parts along dimension 0, may hold values from -6 to 6
Outputs:
- mixed: bfloat16 [64, 256, 2048], P(('parts', 'fsdp', 'dp')), parts along dimension 0
- grad_out: float32 [2048, 2048], P(('parts', 'fsdp', 'dp')), parts along dimension 0
The draws below stay inside these ranges and needn't reach their ends.
There are 2 independent parts, one for each index of `parts`. The reference program is written for one: setup_inputs(seed, part) draws one part's arguments, and reference() takes and returns one part's arrays. A program takes and returns all parts, laid end to end along the dimension named above; an argument that names none is the same for every part. Nothing has to cross between parts.
Inputs may be any that keep to these rules, and one draw needn't show every extreme that they name: `counts`: agents of each scene; some scene has exactly 32 agents and some exactly one. `repack_order`: each row is a permutation of 0 to 3.
All inputs are finite; a program needn't handle non-finite values.
Results may differ from the reference program's by a relative error of at most 0.0077.
Values may be sent and summed in bfloat16 or wider, within the bound.
A program may use at most 128 MiB of HBM per device.

```python
import math
import jax
import jax.numpy as jnp
from jax import lax

D = 2048
HEADS = 8
HW = 1024
AMAX = 32
TSTEP = 8
SLOT = 256
GROUP = 4
PAIRS = 8
SCENES = 32


def draw_counts(key, part):
    key = jax.random.fold_in(key, 11)
    key_one, key_two, key_three = jax.random.split(key, 3)
    drawn = jax.random.randint(key_one, (SCENES,), 1, AMAX + 1)
    full_spot = jax.random.randint(key_two, (), 0, SCENES)
    single_spot = (full_spot + 1 + jax.random.randint(key_three, (), 0, SCENES - 1)) % SCENES
    drawn = drawn.at[full_spot].set(AMAX).at[single_spot].set(1)
    return drawn.astype(jnp.int32)


def draw_key_shift(key, part):
    key = jax.random.fold_in(key, 23)
    key_one = jax.random.fold_in(key, 0)
    drawn = jnp.clip(jax.random.normal(key_one, (SCENES, HEADS, SLOT), jnp.float32), -6.0, 6.0)
    return drawn.astype(jnp.bfloat16)


def block_levels(stream_key, shape, shards, low, largest):
    factor_of, own = 1.0, jax.random.fold_in(stream_key, 6)
    for dim, blocks in shards:
        heights = jnp.exp(jax.random.uniform(jax.random.fold_in(own, dim), (blocks,), jnp.float32, low / len(shards), largest / len(shards)))
        factor_of = factor_of * jnp.repeat(heights, shape[dim] // blocks).reshape([-1 if axis == dim else 1 for axis in range(len(shape))])
    return factor_of


def bell_draw(stream_key, dims, scale, limit, cuts=(), kind=jnp.bfloat16):
    values = scale * jax.random.normal(stream_key, dims, jnp.float32)
    if cuts:
        values = values * block_levels(stream_key, dims, cuts, -0.22, 0.18)
    return jnp.clip(values, -limit, limit).astype(kind)


def setup_inputs(seed: int = 0, part: int = 0) -> dict:
    streams_of = jax.random.split(jax.random.key(seed), 11)
    part_splits = jax.random.split(jax.random.fold_in(streams_of[10], part), 11)
    return {
        "tokens": bell_draw(part_splits[0], (SCENES, SLOT, D), 1.0, 6.0, ((0, 16),)),
        "key_shift": draw_key_shift(jax.random.fold_in(jax.random.fold_in(streams_of[10], part), 71), part),
        "counts": draw_counts(jax.random.fold_in(jax.random.fold_in(streams_of[10], part), 71), part),
        "repack_order": jax.vmap(lambda own: jax.random.permutation(own, GROUP))(jax.random.split(part_splits[3], PAIRS)).reshape((PAIRS, GROUP)).astype(jnp.int32),
        "norm_gain": jnp.clip(1.0 + 0.1 * jax.random.normal(streams_of[4], (D,), jnp.float32), 0.5, 1.5),
        "query_weight": bell_draw(streams_of[5], (D, HW), D ** -0.5, 0.125, ((0, 8),)),
        "key_weight": bell_draw(streams_of[6], (D, HW), D ** -0.5, 0.125, ((0, 8),)),
        "value_weight": bell_draw(streams_of[7], (D, HW), D ** -0.5, 0.125, ((0, 8),)),
        "out_weight": bell_draw(streams_of[8], (HW, D), HW ** -0.5, 0.1875, ((0, 8),)),
        "cotangent": bell_draw(part_splits[9], (SCENES, SLOT, D), 1.0, 6.0, ((0, 16),)),
    }


def attend(queries, key_rows, values, key_shift, live_counts):
    scene_count, slot_rows, proj_width = queries.shape
    head_count = key_shift.shape[1]
    head_dim = proj_width // head_count
    split_shape = (scene_count, slot_rows, head_count, head_dim)
    query_heads = queries.astype(jnp.float32).reshape(split_shape)
    key_heads = key_rows.astype(jnp.float32).reshape(split_shape)
    value_heads = values.astype(jnp.float32).reshape(split_shape)
    scores = jnp.einsum('bqhe,bkhe->bhqk', query_heads, key_heads) * (1.0 / math.sqrt(head_dim))
    scores = scores + key_shift.astype(jnp.float32)[:, :, None, :]
    position = jnp.arange(slot_rows, dtype=jnp.int32)
    moment = position % TSTEP
    agent_index = position // TSTEP
    causal = (moment[None, :] <= moment[:, None])[None, None, :, :]
    present = (agent_index[None, :] < live_counts[:, None])[:, None, None, :]
    scores = jnp.where(causal & present, scores, -1e+30)
    row_max = lax.optimization_barrier(jnp.max(scores, axis=-1, keepdims=True))
    weights = jnp.exp(scores - row_max)
    probabilities = (weights / lax.optimization_barrier(jnp.sum(weights, axis=-1, keepdims=True))).astype(jnp.bfloat16)
    attended = jnp.einsum('bhqk,bkhe->bqhe', probabilities.astype(jnp.float32), value_heads)
    return attended.reshape(scene_count, slot_rows, proj_width).astype(jnp.bfloat16)

def one_scene(scene_items):
    return attend(scene_items[0][None], scene_items[1][None], scene_items[2][None], scene_items[3][None], scene_items[4][None])[0]

def reference(tokens, key_shift, counts, repack_order, norm_gain, query_weight, key_weight, value_weight, out_weight, cotangent):
    group_size = repack_order.shape[1]
    source = (jnp.arange(repack_order.shape[0], dtype=jnp.int32)[:, None] * group_size + repack_order).reshape(-1).astype(jnp.int32)
    packed = tokens[source]
    shifts = key_shift[source]
    live_counts = counts[source]
    floats = packed.astype(jnp.float32).reshape(-1, D)
    normed = (floats * lax.rsqrt(lax.optimization_barrier(jnp.mean(floats * floats, axis=-1, keepdims=True)) + 1e-05) * norm_gain).astype(jnp.bfloat16)
    queries = jnp.dot(normed, query_weight, preferred_element_type=jnp.float32).astype(jnp.bfloat16).reshape(SCENES, SLOT, HW)
    key_rows = jnp.dot(normed, key_weight, preferred_element_type=jnp.float32).astype(jnp.bfloat16).reshape(SCENES, SLOT, HW)
    values = jnp.dot(normed, value_weight, preferred_element_type=jnp.float32).astype(jnp.bfloat16).reshape(SCENES, SLOT, HW)
    attended = lax.map(one_scene, (queries, key_rows, values, shifts, live_counts))
    attended_flat = attended.reshape(-1, HW)
    branch = jnp.dot(attended_flat, out_weight, preferred_element_type=jnp.float32)
    mixed = (floats + branch).astype(jnp.bfloat16).reshape(SCENES, SLOT, D)
    product = lax.dot_general(attended_flat, cotangent.reshape(-1, D), (((0,), (0,)), ((), ())), preferred_element_type=jnp.float32)
    grad_out = product * (1.0 / math.sqrt(SCENES * SLOT))
    return (mixed, grad_out)
```

```python
import functools
import math

import jax
import jax.numpy as jnp
from jax import lax
from jax.experimental import pallas as pl
from jax.experimental.pallas import tpu as pltpu
from jax.sharding import PartitionSpec as P

TSTEP = 8
WIDE = 512
MESH = pl.DeviceIdType.MESH
BF16, F32 = jnp.bfloat16, jnp.float32


def cut(rows):
    return max(16, rows * 5 // 16 // 16 * 16)


def kernel(
    n, heads,
    order_ref, counts_ref, gain_ref, tok_ref, shift_ref, wq_ref, wk_ref, wv_ref, wo_ref, cot_ref,
    mixed_ref, grad_ref,
    held, heldshift, shf, normed, buf, obuf, acc, att, cot, gmine, gsend, gsib, rrecv, rsend,
    mixs, gout,
    loc_sem, tok_sem, out_sem,
    a_ring, a_sib, a_x, a_sibx,
    b_ring, b_sib, b_x, b_sibx,
    gs_sem, r_sem,
):
    dp, fs, part = lax.axis_index("dp"), lax.axis_index("fsdp"), lax.axis_index("parts")
    rows = normed.shape[2]
    orows = wo_ref.shape[0]
    pa, pb = buf.shape[0] // 2, obuf.shape[0] // 2
    ma, mb = (n - 1) * pa, (n - 1) * pb
    tok_rows = normed.shape[1]
    slot = tok_rows // 2
    hd = att.shape[1] // heads
    rp = gmine.shape[2]
    gp = gmine.shape[1]
    rem, div = lax.rem, lax.div

    half = n // 2
    side = rem(fs, 2)
    r = (1 - side) * div(fs, 2) + side * (n - 1 - div(fs, 2))
    way = 1 - 2 * dp

    def at(q):
        q = rem(q + n, n)
        back = div(q, half)
        return (1 - back) * 2 * q + back * (2 * (n - 1 - q) + 1)

    nxt = {"fsdp": at(r + way)}
    prv = {"fsdp": at(r - way)}
    sib = {"dp": 1 - dp}
    xp = rem(part, 2)
    xdev = {"parts": part + 1 - 2 * xp}

    barrier = pltpu.get_barrier_semaphore()
    for dev in (nxt, prv, sib, xdev):
        pl.semaphore_signal(barrier, inc=1, device_id=dev, device_id_type=MESH)
    pl.semaphore_wait(barrier, 4)

    def rcopy(src, dst, sems, i, dev):
        return pltpu.make_async_remote_copy(
            src_ref=src, dst_ref=dst, send_sem=sems.at[0, i], recv_sem=sems.at[1, i],
            device_id=dev, device_id_type=MESH,
        )

    def part_rows(height):
        a = cut(height)
        ring = (a * xp, height - a)
        mine = ((height - a) * xp, a)
        other = ((height - a) * (1 - xp), a)
        return ring, mine, other

    def piece(ref, p, owner, height, span):
        start = pl.multiple_of(owner * height + span[0], 16)
        return ref.at[p, pl.ds(start, span[1]), :]

    ring_a, mine_a, other_a = part_rows(rows)
    ring_b, mine_b, other_b = part_rows(orows)

    class Gather:
        def __init__(self, ref, height, count, spans, ring, sibl, x, sibx):
            self.ref, self.height, self.count = ref, height, count
            self.ring_rows, self.mine, self.other = spans
            self.ring, self.sibl, self.x, self.sibx = ring, sibl, x, sibx
            self.total = (n - 1) * count

        def here(self, m):
            return at(r - way * (div(m, self.count) + 1)), dp * self.count + rem(m, self.count)

        def there(self, m):
            return at(r + way * (div(m, self.count) + 1)), (1 - dp) * self.count + rem(m, self.count)

        def cp(self, kind, m, where):
            owner, p = where
            span, sems, dev = {
                "ring": (self.ring_rows, self.ring, nxt),
                "sib": (self.ring_rows, self.sibl, sib),
                "x": (self.mine, self.x, xdev),
                "xin": (self.other, self.x, xdev),
                "sibx": (self.other, self.sibx, sib),
            }[kind]
            ref = piece(self.ref, p, owner, self.height, span)
            return rcopy(ref, ref, sems, m, dev)

        def step(self, m):
            w = self.here(m)
            self.cp("ring", m, w).wait_recv()

            @pl.when(m < self.total - self.count)
            def _():
                self.cp("ring", m + self.count, w).start()

            self.cp("x", m, w).start()
            self.cp("sib", m, w).start()

        def step_x(self, m):
            w = self.here(m)
            self.cp("xin", m, w).wait_recv()
            self.cp("sibx", m, w).start()

        def arrived(self, m):
            w = self.there(m)
            self.cp("sib", m, w).wait_recv()
            self.cp("sibx", m, w).wait_recv()

        def drain(self):
            @pl.loop(0, self.total)
            def _(m):
                w = self.here(m)
                self.cp("ring", m, w).wait_send()
                self.cp("x", m, w).wait_send()
                self.cp("sib", m, w).wait_send()
                self.cp("sibx", m, w).wait_send()

    ga = Gather(buf, rows, pa, (ring_a, mine_a, other_a), a_ring, a_sib, a_x, a_sibx)
    gb = Gather(obuf, orows, pb, (ring_b, mine_b, other_b), b_ring, b_sib, b_x, b_sibx)

    def own_cols(j):
        return pl.ds(pl.multiple_of((dp * pb + j) * WIDE, WIDE), WIDE)

    weights = (wq_ref, wk_ref, wv_ref)
    for j in range(pa):
        cols = pl.ds(pl.multiple_of(dp * WIDE, WIDE), WIDE)
        src = weights[j].at[pl.ds(pl.multiple_of(ring_a[0], 16), ring_a[1]), cols]
        dst = piece(buf, dp * pa + j, fs, rows, ring_a)
        rcopy(src, dst, a_ring, j, nxt).start()

    tok_in = held.at[pl.ds(dp * 2, 2)]
    tcopy = rcopy(tok_ref, tok_in, tok_sem, 0, sib)
    tcopy.start()
    scopy = rcopy(shift_ref, heldshift.at[dp], tok_sem, 1, sib)
    scopy.start()

    local = []

    def lcopy(src, dst):
        c = pltpu.make_async_copy(src, dst, loc_sem.at[len(local)])
        c.start()
        local.append(c)

    lcopy(tok_ref, tok_in)
    lcopy(shift_ref, heldshift.at[dp])
    for d in range(2):
        for j in range(pa):
            lcopy(
                weights[j].at[:, pl.ds(d * WIDE, WIDE)],
                piece(buf, d * pa + j, fs, rows, (0, rows)),
            )
    for p in range(2 * pb):
        lcopy(wo_ref.at[:, pl.ds(p * WIDE, WIDE)], piece(obuf, p, fs, orows, (0, orows)))
    lcopy(cot_ref, cot)

    def add(owner, p, first=False):
        start = pl.multiple_of(owner * rows, 16)
        term = jnp.dot(
            normed[owner], buf[p, pl.ds(start, rows), :], preferred_element_type=F32
        )
        if first:
            acc[p] = term
        else:
            acc[p] += term

    def add_here(m):
        add(*ga.here(m))

    def add_there(m):
        ga.arrived(m)
        add(*ga.there(m))

    lead = 2 * pa

    @pl.loop(0, lead)
    def _(m):
        ga.step(m)

        @pl.when(m >= 1)
        def _():
            ga.step_x(m - 1)

    for c in local:
        c.wait()
    rcopy(tok_ref, held.at[pl.ds(2 - dp * 2, 2)], tok_sem, 0, sib).wait_recv()
    rcopy(shift_ref, heldshift.at[1 - dp], tok_sem, 1, sib).wait_recv()
    for d in range(2):
        shf[pl.ds(d * 16, 16), :] = heldshift[d].astype(F32)

    tile = 32
    per = slot // tile

    @pl.loop(0, 2 * per)
    def _(t):
        k = div(t, per)
        chosen = order_ref[0, dp * 2 + k]
        x = held[chosen, pl.ds(pl.multiple_of(rem(t, per) * tile, tile), tile), :].astype(F32)
        scale = lax.rsqrt(jnp.mean(x * x, axis=-1, keepdims=True) + 1e-05)
        y = (x * scale * gain_ref[...]).astype(BF16)
        at_rows = pl.ds(pl.multiple_of(t * tile, tile), tile)
        for c in range(n):
            normed[c, at_rows, :] = y[:, c * rows:(c + 1) * rows]

    @pl.loop(0, 2 * pa)
    def _(p):
        add(fs, p, True)

    @pl.loop(lead, ma + 2)
    def _(m):
        @pl.when(m < ma)
        def _():
            ga.step(m)

        @pl.when(m == ma - pa)
        def _():
            for j in range(pb):
                ref = piece(obuf, dp * pb + j, fs, orows, ring_b)
                rcopy(ref, ref, b_ring, j, nxt).start()

        @pl.when(m <= ma)
        def _():
            ga.step_x(m - 1)
            add_here(m - 1)

        add_there(m - 2)
        late = m - lead

        @pl.when(late < lead - 1)
        def _():
            add_here(late)

        @pl.when(late < lead - 2)
        def _():
            add_there(late)

    per_half = heads // 2
    per_head = hd // (2 * rp)

    def attend(h, k):
        d = div(h, per_half)
        cols = pl.ds(pl.multiple_of(rem(h, per_half) * hd, hd), hd)
        rws = pl.ds(pl.multiple_of(k * slot, slot), slot)
        q = acc[d * 3, rws, cols].astype(BF16)
        kk = acc[d * 3 + 1, rws, cols].astype(BF16)
        v = acc[d * 3 + 2, rws, cols].astype(BF16)
        chosen = order_ref[0, dp * 2 + k]
        live = counts_ref[fs * 4 + chosen]
        row = shf[pl.ds(chosen * 8 + h, 1), :]
        s = lax.dot_general(q, kk, (((1,), (1,)), ((), ())), preferred_element_type=F32)
        s = s * (1.0 / math.sqrt(hd)) + row
        i = lax.broadcasted_iota(jnp.int32, (slot, slot), 0)
        j = lax.broadcasted_iota(jnp.int32, (slot, slot), 1)
        ok = ((j & (TSTEP - 1)) <= (i & (TSTEP - 1))) & (j < live * TSTEP)
        s = jnp.where(ok, s, -1e30)
        w = jnp.exp(s - jnp.max(s, axis=-1, keepdims=True))
        prob = (w * (1.0 / jnp.sum(w, axis=-1, keepdims=True))).astype(BF16)
        o = jnp.dot(prob, v, preferred_element_type=F32).astype(BF16)
        att[rws, pl.ds(pl.multiple_of(h * hd, hd), hd)] = o

    def gcopy(o):
        return rcopy(gsend.at[o], gsib.at[o], gs_sem, o, sib)

    def gradient(h):
        a = att[:, pl.ds(pl.multiple_of(h * hd, hd), hd)]
        for c in range(gp):
            g = lax.dot_general(
                a, cot[:, c * WIDE:(c + 1) * WIDE], (((0,), (0,)), ((), ())),
                preferred_element_type=F32,
            )
            for o in range(per_head):
                g0 = g[(2 * o) * rp:(2 * o + 1) * rp]
                g1 = g[(2 * o + 1) * rp:(2 * o + 2) * rp]
                gmine[h * per_head + o, c] = jnp.where(dp == 0, g0, g1)
                gsend[h * per_head + o, c] = jnp.where(dp == 0, g1, g0).astype(BF16)
        for o in range(per_head):
            gcopy(h * per_head + o).start()

    @pl.loop(0, max(mb + 1, 2 * heads))
    def _(m):
        @pl.when(m < mb)
        def _():
            gb.step(m)

        @pl.when((m >= 1) & (m <= mb))
        def _():
            gb.step_x(m - 1)

        @pl.when(m < 2 * heads)
        def _():
            attend(div(m, 2), rem(m, 2))

        @pl.when((m < 2 * heads) & (rem(m, 2) == 1))
        def _():
            gradient(div(m, 2))

    @pl.loop(0, mb)
    def _(m):
        gb.arrived(m)

    def mixcopy(k, c):
        cols = pl.ds(pl.multiple_of(c * WIDE, WIDE), WIDE)
        return pltpu.make_async_copy(
            mixs.at[k, :, cols], mixed_ref.at[k, :, cols], out_sem.at[k * 2 * pb + c]
        )

    def mix(t):
        k, c = rem(t, 2), div(t, 2)
        rws = pl.ds(pl.multiple_of(k * slot, slot), slot)
        cols = pl.ds(pl.multiple_of(c * WIDE, WIDE), WIDE)
        branch = jnp.dot(att[rws, :], obuf[c], preferred_element_type=F32)
        chosen = order_ref[0, dp * 2 + k]
        mixs[k, :, cols] = (held[chosen, :, cols].astype(F32) + branch).astype(BF16)
        mixcopy(k, c).start()

    def hop(m):
        return rcopy(rsend.at[m], rrecv.at[m], r_sem, m, nxt)

    scale = 1.0 / math.sqrt(tok_rows * n * 2)

    @pl.loop(0, n * gp)
    def _(m):
        s, c = div(m, gp), rem(m, gp)
        owner = at(r - way * (s + 1))

        @pl.when(c == 0)
        def _():
            gcopy(owner).wait_recv()

        @pl.when(s == 0)
        def _():
            rsend[m] = (gmine[owner, c] + gsib[owner, c].astype(F32)).astype(BF16)
            hop(m).start()

        @pl.when((s > 0) & (s < n - 1))
        def _():
            hop(m - gp).wait_recv()
            rsend[m] = (
                gmine[owner, c] + gsib[owner, c].astype(F32) + rrecv[m - gp].astype(F32)
            ).astype(BF16)
            hop(m).start()

        @pl.when(s == n - 1)
        def _():
            hop(m - gp).wait_recv()
            gout[:, pl.ds(pl.multiple_of(c * WIDE, WIDE), WIDE)] = scale * (
                gmine[owner, c] + gsib[owner, c].astype(F32) + rrecv[m - gp].astype(F32)
            )

        @pl.when((c == gp - 1) & (s < 4 * pb))
        def _():
            mix(s)

    gcp = pltpu.make_async_copy(gout, grad_ref, out_sem.at[4 * pb])
    gcp.start()
    for k in range(2):
        for c in range(2 * pb):
            mixcopy(k, c).wait()

    ga.drain()
    gb.drain()
    tcopy.wait_send()
    scopy.wait_send()

    @pl.loop(0, n)
    def _(o):
        gcopy(o).wait_send()

    @pl.loop(0, (n - 1) * gp)
    def _(m):
        hop(m).wait_send()

    gcp.wait()


def body(n, tokens, key_shift, counts, repack_order, norm_gain, wq, wk, wv, wo, cotangent):
    scenes, slot, width = tokens.shape
    rows, proj = wq.shape
    orows = wo.shape[0]
    heads = key_shift.shape[1]
    tok_rows = scenes * slot
    rp = proj // (2 * n)
    gp = width // WIDE
    pa, pb = 3 * proj // 2 // WIDE, width // 2 // WIDE
    ma, mb = (n - 1) * pa, (n - 1) * pb
    dma = pltpu.SemaphoreType.DMA
    any_spec = pl.BlockSpec(memory_space=pl.ANY)
    smem = pl.BlockSpec(memory_space=pltpu.SMEM)
    vmem = pl.BlockSpec(memory_space=pltpu.VMEM)
    mixed, grad = pl.pallas_call(
        functools.partial(kernel, n, heads),
        out_shape=(
            jax.ShapeDtypeStruct((scenes, slot, width), BF16),
            jax.ShapeDtypeStruct((rp, width), F32),
        ),
        in_specs=[smem, smem, vmem] + [any_spec] * 7,
        out_specs=(any_spec, any_spec),
        scratch_shapes=[
            pltpu.VMEM((2 * scenes, slot, width), BF16),
            pltpu.VMEM((2, scenes * heads, slot), BF16),
            pltpu.VMEM((2 * scenes * heads, slot), F32),
            pltpu.VMEM((n, tok_rows, rows), BF16),
            pltpu.VMEM((2 * pa, n * rows, WIDE), BF16),
            pltpu.VMEM((2 * pb, n * orows, WIDE), BF16),
            pltpu.VMEM((2 * pa, tok_rows, WIDE), F32),
            pltpu.VMEM((tok_rows, proj), BF16),
            pltpu.VMEM((tok_rows, width), BF16),
            pltpu.VMEM((n, gp, rp, WIDE), F32),
            pltpu.VMEM((n, gp, rp, WIDE), BF16),
            pltpu.VMEM((n, gp, rp, WIDE), BF16),
            pltpu.VMEM(((n - 1) * gp, rp, WIDE), BF16),
            pltpu.VMEM(((n - 1) * gp, rp, WIDE), BF16),
            pltpu.VMEM((scenes, slot, width), BF16),
            pltpu.VMEM((rp, width), F32),
            dma((3 + 2 * pa + 2 * pb,)),
            dma((2, 2)),
            dma((4 * pb + 1,)),
            dma((2, ma)), dma((2, ma)), dma((2, ma)), dma((2, ma)),
            dma((2, mb)), dma((2, mb)), dma((2, mb)), dma((2, mb)),
            dma((2, n)),
            dma((2, (n - 1) * gp)),
        ],
        compiler_params=pltpu.CompilerParams(
            collective_id=0, has_side_effects=True, vmem_limit_bytes=60 * 1024 * 1024
        ),
    )(
        repack_order, counts, norm_gain.reshape(1, width), tokens,
        key_shift.reshape(scenes * heads, slot), wq, wk, wv, wo, cotangent.reshape(tok_rows, width),
    )
    return mixed, grad


def solution(mesh):
    return jax.shard_map(
        functools.partial(body, mesh.shape["fsdp"]),
        mesh=mesh,
        in_specs=(
            P(("parts", "fsdp", "dp"), None, None),
            P(("parts", "fsdp", "dp"), None, None),
            P("parts"),
            P(("parts", "fsdp"), None),
            P(),
            P("fsdp", None),
            P("fsdp", None),
            P("fsdp", None),
            P("fsdp", None),
            P(("parts", "fsdp", "dp"), None, None),
        ),
        out_specs=(P(("parts", "fsdp", "dp"), None, None), P(("parts", "fsdp", "dp"), None)),
        check_vma=False,
    )
```

```python
import functools
import math

import jax
import jax.numpy as jnp
from jax import lax
from jax.experimental import pallas as pl
from jax.experimental.pallas import tpu as pltpu
from jax.sharding import PartitionSpec as P

TSTEP = 8
WIDE = 512
MESH = pl.DeviceIdType.MESH
BF16, F32 = jnp.bfloat16, jnp.float32


def cut(rows):
    return max(16, rows * 5 // 16 // 16 * 16)


def kernel(
    n, heads,
    order_ref, counts_ref, gain_ref, tok_ref, shift_ref, wq_ref, wk_ref, wv_ref, wo_ref, cot_ref,
    mixed_ref, grad_ref,
    held, heldshift, shf, normed, buf, obuf, acc, att, cot, gmine, gsend, gsib, rrecv, rsend,
    mixs, gout,
    loc_sem, tok_sem, out_sem,
    a_ring, a_sib, a_x, a_sibx,
    b_ring, b_sib, b_x, b_sibx,
    gs_sem, r_sem,
):
    dp, fs, part = lax.axis_index("dp"), lax.axis_index("fsdp"), lax.axis_index("parts")
    rows = normed.shape[2]
    orows = wo_ref.shape[0]
    pa, pb = buf.shape[0] // 2, obuf.shape[0] // 2
    ma, mb = (n - 1) * pa, (n - 1) * pb
    tok_rows = normed.shape[1]
    slot = tok_rows // 2
    hd = att.shape[1] // heads
    rp = gmine.shape[2]
    gp = gmine.shape[1]
    rem, div = lax.rem, lax.div

    half = n // 2
    side = rem(fs, 2)
    r = (1 - side) * div(fs, 2) + side * (n - 1 - div(fs, 2))
    way = 1 - 2 * dp

    def at(q):
        q = rem(q + n, n)
        back = div(q, half)
        return (1 - back) * 2 * q + back * (2 * (n - 1 - q) + 1)

    nxt = {"fsdp": at(r + way)}
    prv = {"fsdp": at(r - way)}
    sib = {"dp": 1 - dp}
    xp = rem(part, 2)
    xdev = {"parts": part + 1 - 2 * xp}

    barrier = pltpu.get_barrier_semaphore()
    for dev in (nxt, prv, sib, xdev):
        pl.semaphore_signal(barrier, inc=1, device_id=dev, device_id_type=MESH)
    pl.semaphore_wait(barrier, 4)

    def rcopy(src, dst, sems, i, dev):
        return pltpu.make_async_remote_copy(
            src_ref=src, dst_ref=dst, send_sem=sems.at[0, i], recv_sem=sems.at[1, i],
            device_id=dev, device_id_type=MESH,
        )

    def part_rows(height):
        a = cut(height)
        ring = (a * xp, height - a)
        mine = ((height - a) * xp, a)
        other = ((height - a) * (1 - xp), a)
        return ring, mine, other

    def piece(ref, p, owner, height, span):
        start = pl.multiple_of(owner * height + span[0], 16)
        return ref.at[p, pl.ds(start, span[1]), :]

    ring_a, mine_a, other_a = part_rows(rows)
    ring_b, mine_b, other_b = part_rows(orows)

    class Gather:
        def __init__(self, ref, height, count, spans, ring, sibl, x, sibx):
            self.ref, self.height, self.count = ref, height, count
            self.ring_rows, self.mine, self.other = spans
            self.ring, self.sibl, self.x, self.sibx = ring, sibl, x, sibx
            self.total = (n - 1) * count

        def here(self, m):
            return at(r - way * (div(m, self.count) + 1)), dp * self.count + rem(m, self.count)

        def there(self, m):
            return at(r + way * (div(m, self.count) + 1)), (1 - dp) * self.count + rem(m, self.count)

        def cp(self, kind, m, where):
            owner, p = where
            span, sems, dev = {
                "ring": (self.ring_rows, self.ring, nxt),
                "sib": (self.ring_rows, self.sibl, sib),
                "x": (self.mine, self.x, xdev),
                "xin": (self.other, self.x, xdev),
                "sibx": (self.other, self.sibx, sib),
            }[kind]
            ref = piece(self.ref, p, owner, self.height, span)
            return rcopy(ref, ref, sems, m, dev)

        def step(self, m):
            w = self.here(m)
            self.cp("ring", m, w).wait_recv()

            @pl.when(m < self.total - self.count)
            def _():
                self.cp("ring", m + self.count, w).start()

            self.cp("x", m, w).start()
            self.cp("sib", m, w).start()

        def step_x(self, m):
            w = self.here(m)
            self.cp("xin", m, w).wait_recv()
            self.cp("sibx", m, w).start()

        def arrived(self, m):
            w = self.there(m)
            self.cp("sib", m, w).wait_recv()
            self.cp("sibx", m, w).wait_recv()

        def drain(self):
            @pl.loop(0, self.total)
            def _(m):
                w = self.here(m)
                self.cp("ring", m, w).wait_send()
                self.cp("x", m, w).wait_send()
                self.cp("sib", m, w).wait_send()
                self.cp("sibx", m, w).wait_send()

    ga = Gather(buf, rows, pa, (ring_a, mine_a, other_a), a_ring, a_sib, a_x, a_sibx)
    gb = Gather(obuf, orows, pb, (ring_b, mine_b, other_b), b_ring, b_sib, b_x, b_sibx)

    def own_cols(j):
        return pl.ds(pl.multiple_of((dp * pb + j) * WIDE, WIDE), WIDE)

    weights = (wq_ref, wk_ref, wv_ref)
    for j in range(pa):
        cols = pl.ds(pl.multiple_of(dp * WIDE, WIDE), WIDE)
        src = weights[j].at[pl.ds(pl.multiple_of(ring_a[0], 16), ring_a[1]), cols]
        dst = piece(buf, dp * pa + j, fs, rows, ring_a)
        rcopy(src, dst, a_ring, j, nxt).start()

    tok_in = held.at[pl.ds(dp * 2, 2)]
    tcopy = rcopy(tok_ref, tok_in, tok_sem, 0, sib)
    tcopy.start()
    scopy = rcopy(shift_ref, heldshift.at[dp], tok_sem, 1, sib)
    scopy.start()

    local = []

    def lcopy(src, dst):
        c = pltpu.make_async_copy(src, dst, loc_sem.at[len(local)])
        c.start()
        local.append(c)

    lcopy(tok_ref, tok_in)
    lcopy(shift_ref, heldshift.at[dp])
    for d in range(2):
        for j in range(pa):
            lcopy(
                weights[j].at[:, pl.ds(d * WIDE, WIDE)],
                piece(buf, d * pa + j, fs, rows, (0, rows)),
            )
    for p in range(2 * pb):
        lcopy(wo_ref.at[:, pl.ds(p * WIDE, WIDE)], piece(obuf, p, fs, orows, (0, orows)))
    lcopy(cot_ref, cot)

    def add(owner, p, first=False):
        start = pl.multiple_of(owner * rows, 16)
        term = jnp.dot(
            normed[owner], buf[p, pl.ds(start, rows), :], preferred_element_type=F32
        )
        if first:
            acc[p] = term
        else:
            acc[p] += term

    def add_here(m):
        add(*ga.here(m))

    def add_there(m):
        ga.arrived(m)
        add(*ga.there(m))

    lead, lag = 2 * pa, pa

    @pl.loop(0, lead)
    def _(m):
        ga.step(m)

        @pl.when(m >= lag)
        def _():
            ga.step_x(m - lag)

    for c in local:
        c.wait()
    rcopy(tok_ref, held.at[pl.ds(2 - dp * 2, 2)], tok_sem, 0, sib).wait_recv()
    rcopy(shift_ref, heldshift.at[1 - dp], tok_sem, 1, sib).wait_recv()
    for d in range(2):
        shf[pl.ds(d * 16, 16), :] = heldshift[d].astype(F32)

    tile = 32
    per = slot // tile

    @pl.loop(0, 2 * per)
    def _(t):
        k = div(t, per)
        chosen = order_ref[0, dp * 2 + k]
        x = held[chosen, pl.ds(pl.multiple_of(rem(t, per) * tile, tile), tile), :].astype(F32)
        scale = lax.rsqrt(jnp.mean(x * x, axis=-1, keepdims=True) + 1e-05)
        y = (x * scale * gain_ref[...]).astype(BF16)
        at_rows = pl.ds(pl.multiple_of(t * tile, tile), tile)
        for c in range(n):
            normed[c, at_rows, :] = y[:, c * rows:(c + 1) * rows]

    @pl.loop(0, 2 * pa)
    def _(p):
        add(fs, p, True)

    @pl.loop(lead, ma + lag + 1)
    def _(m):
        @pl.when(m < ma)
        def _():
            ga.step(m)

        @pl.when(m == ma - pa)
        def _():
            for j in range(pb):
                ref = piece(obuf, dp * pb + j, fs, orows, ring_b)
                rcopy(ref, ref, b_ring, j, nxt).start()

        @pl.when(m < ma + lag)
        def _():
            ga.step_x(m - lag)
            add_here(m - lag)

        add_there(m - lag - 1)
        late = m - lead

        @pl.when(late < lead - lag)
        def _():
            add_here(late)

        @pl.when(late < lead - lag - 1)
        def _():
            add_there(late)

    per_half = heads // 2
    per_head = hd // (2 * rp)

    def attend(h, k):
        d = div(h, per_half)
        cols = pl.ds(pl.multiple_of(rem(h, per_half) * hd, hd), hd)
        rws = pl.ds(pl.multiple_of(k * slot, slot), slot)
        q = acc[d * 3, rws, cols].astype(BF16)
        kk = acc[d * 3 + 1, rws, cols].astype(BF16)
        v = acc[d * 3 + 2, rws, cols].astype(BF16)
        chosen = order_ref[0, dp * 2 + k]
        live = counts_ref[fs * 4 + chosen]
        row = shf[pl.ds(chosen * 8 + h, 1), :]
        s = lax.dot_general(q, kk, (((1,), (1,)), ((), ())), preferred_element_type=F32)
        s = s * (1.0 / math.sqrt(hd)) + row
        i = lax.broadcasted_iota(jnp.int32, (slot, slot), 0)
        j = lax.broadcasted_iota(jnp.int32, (slot, slot), 1)
        ok = ((j & (TSTEP - 1)) <= (i & (TSTEP - 1))) & (j < live * TSTEP)
        s = jnp.where(ok, s, -1e30)
        w = jnp.exp(s - jnp.max(s, axis=-1, keepdims=True))
        prob = (w * (1.0 / jnp.sum(w, axis=-1, keepdims=True))).astype(BF16)
        o = jnp.dot(prob, v, preferred_element_type=F32).astype(BF16)
        att[rws, pl.ds(pl.multiple_of(h * hd, hd), hd)] = o

    def gcopy(o):
        return rcopy(gsend.at[o], gsib.at[o], gs_sem, o, sib)

    def gradient(h):
        a = att[:, pl.ds(pl.multiple_of(h * hd, hd), hd)]
        for c in range(gp):
            g = lax.dot_general(
                a, cot[:, c * WIDE:(c + 1) * WIDE], (((0,), (0,)), ((), ())),
                preferred_element_type=F32,
            )
            for o in range(per_head):
                g0 = g[(2 * o) * rp:(2 * o + 1) * rp]
                g1 = g[(2 * o + 1) * rp:(2 * o + 2) * rp]
                gmine[h * per_head + o, c] = jnp.where(dp == 0, g0, g1)
                gsend[h * per_head + o, c] = jnp.where(dp == 0, g1, g0).astype(BF16)
        for o in range(per_head):
            gcopy(h * per_head + o).start()

    @pl.loop(0, max(mb + lag, 2 * heads))
    def _(m):
        @pl.when(m < mb)
        def _():
            gb.step(m)

        @pl.when((m >= lag) & (m < mb + lag))
        def _():
            gb.step_x(m - lag)

        @pl.when(m < 2 * heads)
        def _():
            attend(div(m, 2), rem(m, 2))

        @pl.when((m < 2 * heads) & (rem(m, 2) == 1))
        def _():
            gradient(div(m, 2))

    @pl.loop(0, mb)
    def _(m):
        gb.arrived(m)

    def mixcopy(k, c):
        cols = pl.ds(pl.multiple_of(c * WIDE, WIDE), WIDE)
        return pltpu.make_async_copy(
            mixs.at[k, :, cols], mixed_ref.at[k, :, cols], out_sem.at[k * 2 * pb + c]
        )

    def mix(t):
        k, c = rem(t, 2), div(t, 2)
        rws = pl.ds(pl.multiple_of(k * slot, slot), slot)
        cols = pl.ds(pl.multiple_of(c * WIDE, WIDE), WIDE)
        branch = jnp.dot(att[rws, :], obuf[c], preferred_element_type=F32)
        chosen = order_ref[0, dp * 2 + k]
        mixs[k, :, cols] = (held[chosen, :, cols].astype(F32) + branch).astype(BF16)
        mixcopy(k, c).start()

    def hop(m):
        return rcopy(rsend.at[m], rrecv.at[m], r_sem, m, nxt)

    scale = 1.0 / math.sqrt(tok_rows * n * 2)

    @pl.loop(0, n * gp)
    def _(m):
        s, c = div(m, gp), rem(m, gp)
        owner = at(r - way * (s + 1))

        @pl.when(c == 0)
        def _():
            gcopy(owner).wait_recv()

        @pl.when(s == 0)
        def _():
            rsend[m] = (gmine[owner, c] + gsib[owner, c].astype(F32)).astype(BF16)
            hop(m).start()

        @pl.when((s > 0) & (s < n - 1))
        def _():
            hop(m - gp).wait_recv()
            rsend[m] = (
                gmine[owner, c] + gsib[owner, c].astype(F32) + rrecv[m - gp].astype(F32)
            ).astype(BF16)
            hop(m).start()

        @pl.when(s == n - 1)
        def _():
            hop(m - gp).wait_recv()
            gout[:, pl.ds(pl.multiple_of(c * WIDE, WIDE), WIDE)] = scale * (
                gmine[owner, c] + gsib[owner, c].astype(F32) + rrecv[m - gp].astype(F32)
            )

        @pl.when((c == gp - 1) & (s < 4 * pb))
        def _():
            mix(s)

    gcp = pltpu.make_async_copy(gout, grad_ref, out_sem.at[4 * pb])
    gcp.start()
    for k in range(2):
        for c in range(2 * pb):
            mixcopy(k, c).wait()

    ga.drain()
    gb.drain()
    tcopy.wait_send()
    scopy.wait_send()

    @pl.loop(0, n)
    def _(o):
        gcopy(o).wait_send()

    @pl.loop(0, (n - 1) * gp)
    def _(m):
        hop(m).wait_send()

    gcp.wait()


def body(n, tokens, key_shift, counts, repack_order, norm_gain, wq, wk, wv, wo, cotangent):
    scenes, slot, width = tokens.shape
    rows, proj = wq.shape
    orows = wo.shape[0]
    heads = key_shift.shape[1]
    tok_rows = scenes * slot
    rp = proj // (2 * n)
    gp = width // WIDE
    pa, pb = 3 * proj // 2 // WIDE, width // 2 // WIDE
    ma, mb = (n - 1) * pa, (n - 1) * pb
    dma = pltpu.SemaphoreType.DMA
    any_spec = pl.BlockSpec(memory_space=pl.ANY)
    smem = pl.BlockSpec(memory_space=pltpu.SMEM)
    vmem = pl.BlockSpec(memory_space=pltpu.VMEM)
    mixed, grad = pl.pallas_call(
        functools.partial(kernel, n, heads),
        out_shape=(
            jax.ShapeDtypeStruct((scenes, slot, width), BF16),
            jax.ShapeDtypeStruct((rp, width), F32),
        ),
        in_specs=[smem, smem, vmem] + [any_spec] * 7,
        out_specs=(any_spec, any_spec),
        scratch_shapes=[
            pltpu.VMEM((2 * scenes, slot, width), BF16),
            pltpu.VMEM((2, scenes * heads, slot), BF16),
            pltpu.VMEM((2 * scenes * heads, slot), F32),
            pltpu.VMEM((n, tok_rows, rows), BF16),
            pltpu.VMEM((2 * pa, n * rows, WIDE), BF16),
            pltpu.VMEM((2 * pb, n * orows, WIDE), BF16),
            pltpu.VMEM((2 * pa, tok_rows, WIDE), F32),
            pltpu.VMEM((tok_rows, proj), BF16),
            pltpu.VMEM((tok_rows, width), BF16),
            pltpu.VMEM((n, gp, rp, WIDE), F32),
            pltpu.VMEM((n, gp, rp, WIDE), BF16),
            pltpu.VMEM((n, gp, rp, WIDE), BF16),
            pltpu.VMEM(((n - 1) * gp, rp, WIDE), BF16),
            pltpu.VMEM(((n - 1) * gp, rp, WIDE), BF16),
            pltpu.VMEM((scenes, slot, width), BF16),
            pltpu.VMEM((rp, width), F32),
            dma((3 + 2 * pa + 2 * pb,)),
            dma((2, 2)),
            dma((4 * pb + 1,)),
            dma((2, ma)), dma((2, ma)), dma((2, ma)), dma((2, ma)),
            dma((2, mb)), dma((2, mb)), dma((2, mb)), dma((2, mb)),
            dma((2, n)),
            dma((2, (n - 1) * gp)),
        ],
        compiler_params=pltpu.CompilerParams(
            collective_id=0, has_side_effects=True, vmem_limit_bytes=60 * 1024 * 1024
        ),
    )(
        repack_order, counts, norm_gain.reshape(1, width), tokens,
        key_shift.reshape(scenes * heads, slot), wq, wk, wv, wo, cotangent.reshape(tok_rows, width),
    )
    return mixed, grad


def solution(mesh):
    return jax.shard_map(
        functools.partial(body, mesh.shape["fsdp"]),
        mesh=mesh,
        in_specs=(
            P(("parts", "fsdp", "dp"), None, None),
            P(("parts", "fsdp", "dp"), None, None),
            P("parts"),
            P(("parts", "fsdp"), None),
            P(),
            P("fsdp", None),
            P("fsdp", None),
            P("fsdp", None),
            P("fsdp", None),
            P(("parts", "fsdp", "dp"), None, None),
        ),
        out_specs=(P(("parts", "fsdp", "dp"), None, None), P(("parts", "fsdp", "dp"), None)),
        check_vma=False,
    )
```

```python
import functools
import math

import jax
import jax.numpy as jnp
from jax import lax
from jax.experimental import pallas as pl
from jax.experimental.pallas import tpu as pltpu
from jax.sharding import PartitionSpec as P

TSTEP = 8
WIDE = 512
MESH = pl.DeviceIdType.MESH
BF16, F32 = jnp.bfloat16, jnp.float32


def cut(rows):
    return max(16, rows * 5 // 16 // 16 * 16)


def kernel(
    n, heads,
    order_ref, counts_ref, gain_ref, tok_ref, shift_ref, wq_ref, wk_ref, wv_ref, wo_ref, cot_ref,
    mixed_ref, grad_ref,
    held, heldshift, shf, normed, buf, obuf, acc, att, cot, gmine, gsend, gsib, rrecv, rsend,
    mixs, gout,
    loc_sem, tok_sem, out_sem,
    a_ring, a_sib, a_x, a_sibx,
    b_ring, b_sib, b_x, b_sibx,
    gs_sem, r_sem,
):
    dp, fs, part = lax.axis_index("dp"), lax.axis_index("fsdp"), lax.axis_index("parts")
    rows = normed.shape[2]
    orows = wo_ref.shape[0]
    pa, pb = buf.shape[0] // 2, obuf.shape[0] // 2
    ma, mb = (n - 1) * pa, (n - 1) * pb
    tok_rows = normed.shape[1]
    slot = tok_rows // 2
    hd = att.shape[1] // heads
    rp = gmine.shape[2]
    gp = gmine.shape[1]
    rem, div = lax.rem, lax.div

    half = n // 2
    side = rem(fs, 2)
    r = (1 - side) * div(fs, 2) + side * (n - 1 - div(fs, 2))
    way = 1 - 2 * dp

    def at(q):
        q = rem(q + n, n)
        back = div(q, half)
        return (1 - back) * 2 * q + back * (2 * (n - 1 - q) + 1)

    nxt = {"fsdp": at(r + way)}
    prv = {"fsdp": at(r - way)}
    sib = {"dp": 1 - dp}
    xp = rem(part, 2)
    xdev = {"parts": part + 1 - 2 * xp}

    barrier = pltpu.get_barrier_semaphore()
    for dev in (nxt, prv, sib, xdev):
        pl.semaphore_signal(barrier, inc=1, device_id=dev, device_id_type=MESH)
    pl.semaphore_wait(barrier, 4)

    def rcopy(src, dst, sems, i, dev):
        return pltpu.make_async_remote_copy(
            src_ref=src, dst_ref=dst, send_sem=sems.at[0, i], recv_sem=sems.at[1, i],
            device_id=dev, device_id_type=MESH,
        )

    def part_rows(height):
        a = cut(height)
        ring = (a * xp, height - a)
        mine = ((height - a) * xp, a)
        other = ((height - a) * (1 - xp), a)
        return ring, mine, other

    def piece(ref, p, owner, height, span):
        start = pl.multiple_of(owner * height + span[0], 16)
        return ref.at[p, pl.ds(start, span[1]), :]

    ring_a, mine_a, other_a = part_rows(rows)
    ring_b, mine_b, other_b = part_rows(orows)

    class Gather:
        def __init__(self, ref, height, count, spans, ring, sibl, x, sibx):
            self.ref, self.height, self.count = ref, height, count
            self.ring_rows, self.mine, self.other = spans
            self.ring, self.sibl, self.x, self.sibx = ring, sibl, x, sibx
            self.total = (n - 1) * count

        def here(self, m):
            return at(r - way * (div(m, self.count) + 1)), dp * self.count + rem(m, self.count)

        def there(self, m):
            return at(r + way * (div(m, self.count) + 1)), (1 - dp) * self.count + rem(m, self.count)

        def cp(self, kind, m, where):
            owner, p = where
            span, sems, dev = {
                "ring": (self.ring_rows, self.ring, nxt),
                "sib": (self.ring_rows, self.sibl, sib),
                "x": (self.mine, self.x, xdev),
                "xin": (self.other, self.x, xdev),
                "sibx": (self.other, self.sibx, sib),
            }[kind]
            ref = piece(self.ref, p, owner, self.height, span)
            return rcopy(ref, ref, sems, m, dev)

        def step(self, m):
            w = self.here(m)
            self.cp("ring", m, w).wait_recv()

            @pl.when(m < self.total - self.count)
            def _():
                self.cp("ring", m + self.count, w).start()

            self.cp("x", m, w).start()
            self.cp("sib", m, w).start()

        def step_x(self, m):
            w = self.here(m)
            self.cp("xin", m, w).wait_recv()
            self.cp("sibx", m, w).start()

        def arrived(self, m):
            w = self.there(m)
            self.cp("sib", m, w).wait_recv()
            self.cp("sibx", m, w).wait_recv()

        def drain(self):
            @pl.loop(0, self.total)
            def _(m):
                w = self.here(m)
                self.cp("ring", m, w).wait_send()
                self.cp("x", m, w).wait_send()
                self.cp("sib", m, w).wait_send()
                self.cp("sibx", m, w).wait_send()

    ga = Gather(buf, rows, pa, (ring_a, mine_a, other_a), a_ring, a_sib, a_x, a_sibx)
    gb = Gather(obuf, orows, pb, (ring_b, mine_b, other_b), b_ring, b_sib, b_x, b_sibx)

    def own_cols(j):
        return pl.ds(pl.multiple_of((dp * pb + j) * WIDE, WIDE), WIDE)

    weights = (wq_ref, wk_ref, wv_ref)
    for j in range(pa):
        cols = pl.ds(pl.multiple_of(dp * WIDE, WIDE), WIDE)
        src = weights[j].at[pl.ds(pl.multiple_of(ring_a[0], 16), ring_a[1]), cols]
        dst = piece(buf, dp * pa + j, fs, rows, ring_a)
        rcopy(src, dst, a_ring, j, nxt).start()

    tok_in = held.at[pl.ds(dp * 2, 2)]
    tcopy = rcopy(tok_ref, tok_in, tok_sem, 0, sib)
    tcopy.start()
    scopy = rcopy(shift_ref, heldshift.at[dp], tok_sem, 1, sib)
    scopy.start()

    local = []

    def lcopy(src, dst):
        c = pltpu.make_async_copy(src, dst, loc_sem.at[len(local)])
        c.start()
        local.append(c)

    lcopy(tok_ref, tok_in)
    lcopy(shift_ref, heldshift.at[dp])
    for d in range(2):
        for j in range(pa):
            lcopy(
                weights[j].at[:, pl.ds(d * WIDE, WIDE)],
                piece(buf, d * pa + j, fs, rows, (0, rows)),
            )
    for p in range(2 * pb):
        lcopy(wo_ref.at[:, pl.ds(p * WIDE, WIDE)], piece(obuf, p, fs, orows, (0, orows)))
    lcopy(cot_ref, cot)

    def add(owner, p, first=False):
        start = pl.multiple_of(owner * rows, 16)
        term = jnp.dot(
            normed[owner], buf[p, pl.ds(start, rows), :], preferred_element_type=F32
        )
        if first:
            acc[p] = term
        else:
            acc[p] += term

    def add_here(m):
        add(*ga.here(m))

    def add_there(m):
        ga.arrived(m)
        add(*ga.there(m))

    lead, lag = 2 * pa, pa
    join = 3 * pa
    early = pb * (n - 4)

    def tick(b):
        @pl.when(b < mb)
        def _():
            gb.step(b)

        @pl.when((b >= lag) & (b < mb + lag))
        def _():
            gb.step_x(b - lag)


    @pl.loop(0, lead)
    def _(m):
        ga.step(m)

        @pl.when(m >= lag)
        def _():
            ga.step_x(m - lag)

    for c in local:
        c.wait()
    rcopy(tok_ref, held.at[pl.ds(2 - dp * 2, 2)], tok_sem, 0, sib).wait_recv()
    rcopy(shift_ref, heldshift.at[1 - dp], tok_sem, 1, sib).wait_recv()
    for d in range(2):
        shf[pl.ds(d * 16, 16), :] = heldshift[d].astype(F32)

    tile = 32
    per = slot // tile

    @pl.loop(0, 2 * per)
    def _(t):
        k = div(t, per)
        chosen = order_ref[0, dp * 2 + k]
        x = held[chosen, pl.ds(pl.multiple_of(rem(t, per) * tile, tile), tile), :].astype(F32)
        scale = lax.rsqrt(jnp.mean(x * x, axis=-1, keepdims=True) + 1e-05)
        y = (x * scale * gain_ref[...]).astype(BF16)
        at_rows = pl.ds(pl.multiple_of(t * tile, tile), tile)
        for c in range(n):
            normed[c, at_rows, :] = y[:, c * rows:(c + 1) * rows]

    @pl.loop(0, 2 * pa)
    def _(p):
        add(fs, p, True)

    @pl.loop(lead, ma + lag + 1)
    def _(m):
        @pl.when(m < ma)
        def _():
            ga.step(m)

        @pl.when(m == join - pa)
        def _():
            for j in range(pb):
                ref = piece(obuf, dp * pb + j, fs, orows, ring_b)
                rcopy(ref, ref, b_ring, j, nxt).start()

        over = m - join

        @pl.when((over >= 0) & (m < ma) & (rem(over, pa) < pb))
        def _():
            tick(div(over, pa) * pb + rem(over, pa))

        @pl.when(m < ma + lag)
        def _():
            ga.step_x(m - lag)
            add_here(m - lag)

        add_there(m - lag - 1)
        late = m - lead

        @pl.when(late < lead - lag)
        def _():
            add_here(late)

        @pl.when(late < lead - lag - 1)
        def _():
            add_there(late)

    per_half = heads // 2
    per_head = hd // (2 * rp)

    def attend(h, k):
        d = div(h, per_half)
        cols = pl.ds(pl.multiple_of(rem(h, per_half) * hd, hd), hd)
        rws = pl.ds(pl.multiple_of(k * slot, slot), slot)
        q = acc[d * 3, rws, cols].astype(BF16)
        kk = acc[d * 3 + 1, rws, cols].astype(BF16)
        v = acc[d * 3 + 2, rws, cols].astype(BF16)
        chosen = order_ref[0, dp * 2 + k]
        live = counts_ref[fs * 4 + chosen]
        row = shf[pl.ds(chosen * 8 + h, 1), :]
        s = lax.dot_general(q, kk, (((1,), (1,)), ((), ())), preferred_element_type=F32)
        s = s * (1.0 / math.sqrt(hd)) + row
        i = lax.broadcasted_iota(jnp.int32, (slot, slot), 0)
        j = lax.broadcasted_iota(jnp.int32, (slot, slot), 1)
        ok = ((j & (TSTEP - 1)) <= (i & (TSTEP - 1))) & (j < live * TSTEP)
        s = jnp.where(ok, s, -1e30)
        w = jnp.exp(s - jnp.max(s, axis=-1, keepdims=True))
        prob = (w * (1.0 / jnp.sum(w, axis=-1, keepdims=True))).astype(BF16)
        o = jnp.dot(prob, v, preferred_element_type=F32).astype(BF16)
        att[rws, pl.ds(pl.multiple_of(h * hd, hd), hd)] = o

    def gcopy(o):
        return rcopy(gsend.at[o], gsib.at[o], gs_sem, o, sib)

    def gradient(h):
        a = att[:, pl.ds(pl.multiple_of(h * hd, hd), hd)]
        for c in range(gp):
            g = lax.dot_general(
                a, cot[:, c * WIDE:(c + 1) * WIDE], (((0,), (0,)), ((), ())),
                preferred_element_type=F32,
            )
            for o in range(per_head):
                g0 = g[(2 * o) * rp:(2 * o + 1) * rp]
                g1 = g[(2 * o + 1) * rp:(2 * o + 2) * rp]
                gmine[h * per_head + o, c] = jnp.where(dp == 0, g0, g1)
                gsend[h * per_head + o, c] = jnp.where(dp == 0, g1, g0).astype(BF16)
        for o in range(per_head):
            gcopy(h * per_head + o).start()

    def mixcopy(k, c):
        cols = pl.ds(pl.multiple_of(c * WIDE, WIDE), WIDE)
        return pltpu.make_async_copy(
            mixs.at[k, :, cols], mixed_ref.at[k, :, cols], out_sem.at[k * 2 * pb + c]
        )

    def mix(t):
        k, c = rem(t, 2), div(t, 2)
        rws = pl.ds(pl.multiple_of(k * slot, slot), slot)
        cols = pl.ds(pl.multiple_of(c * WIDE, WIDE), WIDE)
        branch = jnp.dot(att[rws, :], obuf[c], preferred_element_type=F32)
        chosen = order_ref[0, dp * 2 + k]
        mixs[k, :, cols] = (held[chosen, :, cols].astype(F32) + branch).astype(BF16)
        mixcopy(k, c).start()

    def hop(m):
        return rcopy(rsend.at[m], rrecv.at[m], r_sem, m, nxt)

    scale = 1.0 / math.sqrt(tok_rows * n * 2)

    def reduce_step(m):
        s, c = div(m, gp), rem(m, gp)
        owner = at(r - way * (s + 1))

        @pl.when(c == 0)
        def _():
            gcopy(owner).wait_recv()

        @pl.when(s == 0)
        def _():
            rsend[m] = (gmine[owner, c] + gsib[owner, c].astype(F32)).astype(BF16)
            hop(m).start()

        @pl.when((s > 0) & (s < n - 1))
        def _():
            hop(m - gp).wait_recv()
            rsend[m] = (
                gmine[owner, c] + gsib[owner, c].astype(F32) + rrecv[m - gp].astype(F32)
            ).astype(BF16)
            hop(m).start()

        @pl.when(s == n - 1)
        def _():
            hop(m - gp).wait_recv()
            gout[:, pl.ds(pl.multiple_of(c * WIDE, WIDE), WIDE)] = scale * (
                gmine[owner, c] + gsib[owner, c].astype(F32) + rrecv[m - gp].astype(F32)
            )

    units = 2 * heads
    matched = n == heads
    ahead = 6
    begun = units - ahead if matched else 0

    def head_at(i):
        if not matched:
            return i
        return at(r + (2 * rem(i, 2) - 1) * (div(i, 2) + 1) - div(i, n - 1) * (n // 2))

    @pl.loop(0, max(mb - early + lag, units))
    def _(u):
        tick(early + u)

        if matched:
            @pl.when((u >= ahead) & (u < units))
            def _():
                reduce_step(u - ahead)

        @pl.when(u < units)
        def _():
            attend(head_at(div(u, 2)), rem(u, 2))

        @pl.when((u < units) & (rem(u, 2) == 1))
        def _():
            gradient(head_at(div(u, 2)))

    @pl.loop(0, mb)
    def _(m):
        gb.arrived(m)

    @pl.loop(begun, n * gp)
    def _(m):
        reduce_step(m)
        past = m - begun

        @pl.when((rem(past, 2) == 0) & (past < 8 * pb))
        def _():
            mix(div(past, 2))

    gcp = pltpu.make_async_copy(gout, grad_ref, out_sem.at[4 * pb])
    gcp.start()
    for k in range(2):
        for c in range(2 * pb):
            mixcopy(k, c).wait()

    ga.drain()
    gb.drain()
    tcopy.wait_send()
    scopy.wait_send()

    @pl.loop(0, n)
    def _(o):
        gcopy(o).wait_send()

    @pl.loop(0, (n - 1) * gp)
    def _(m):
        hop(m).wait_send()

    gcp.wait()


def body(n, tokens, key_shift, counts, repack_order, norm_gain, wq, wk, wv, wo, cotangent):
    scenes, slot, width = tokens.shape
    rows, proj = wq.shape
    orows = wo.shape[0]
    heads = key_shift.shape[1]
    tok_rows = scenes * slot
    rp = proj // (2 * n)
    gp = width // WIDE
    pa, pb = 3 * proj // 2 // WIDE, width // 2 // WIDE
    ma, mb = (n - 1) * pa, (n - 1) * pb
    dma = pltpu.SemaphoreType.DMA
    any_spec = pl.BlockSpec(memory_space=pl.ANY)
    smem = pl.BlockSpec(memory_space=pltpu.SMEM)
    vmem = pl.BlockSpec(memory_space=pltpu.VMEM)
    mixed, grad = pl.pallas_call(
        functools.partial(kernel, n, heads),
        out_shape=(
            jax.ShapeDtypeStruct((scenes, slot, width), BF16),
            jax.ShapeDtypeStruct((rp, width), F32),
        ),
        in_specs=[smem, smem, vmem] + [any_spec] * 7,
        out_specs=(any_spec, any_spec),
        scratch_shapes=[
            pltpu.VMEM((2 * scenes, slot, width), BF16),
            pltpu.VMEM((2, scenes * heads, slot), BF16),
            pltpu.VMEM((2 * scenes * heads, slot), F32),
            pltpu.VMEM((n, tok_rows, rows), BF16),
            pltpu.VMEM((2 * pa, n * rows, WIDE), BF16),
            pltpu.VMEM((2 * pb, n * orows, WIDE), BF16),
            pltpu.VMEM((2 * pa, tok_rows, WIDE), F32),
            pltpu.VMEM((tok_rows, proj), BF16),
            pltpu.VMEM((tok_rows, width), BF16),
            pltpu.VMEM((n, gp, rp, WIDE), F32),
            pltpu.VMEM((n, gp, rp, WIDE), BF16),
            pltpu.VMEM((n, gp, rp, WIDE), BF16),
            pltpu.VMEM(((n - 1) * gp, rp, WIDE), BF16),
            pltpu.VMEM(((n - 1) * gp, rp, WIDE), BF16),
            pltpu.VMEM((scenes, slot, width), BF16),
            pltpu.VMEM((rp, width), F32),
            dma((3 + 2 * pa + 2 * pb,)),
            dma((2, 2)),
            dma((4 * pb + 1,)),
            dma((2, ma)), dma((2, ma)), dma((2, ma)), dma((2, ma)),
            dma((2, mb)), dma((2, mb)), dma((2, mb)), dma((2, mb)),
            dma((2, n)),
            dma((2, (n - 1) * gp)),
        ],
        compiler_params=pltpu.CompilerParams(
            collective_id=0, has_side_effects=True, vmem_limit_bytes=60 * 1024 * 1024
        ),
    )(
        repack_order, counts, norm_gain.reshape(1, width), tokens,
        key_shift.reshape(scenes * heads, slot), wq, wk, wv, wo, cotangent.reshape(tok_rows, width),
    )
    return mixed, grad


def solution(mesh):
    return jax.shard_map(
        functools.partial(body, mesh.shape["fsdp"]),
        mesh=mesh,
        in_specs=(
            P(("parts", "fsdp", "dp"), None, None),
            P(("parts", "fsdp", "dp"), None, None),
            P("parts"),
            P(("parts", "fsdp"), None),
            P(),
            P("fsdp", None),
            P("fsdp", None),
            P("fsdp", None),
            P("fsdp", None),
            P(("parts", "fsdp", "dp"), None, None),
        ),
        out_specs=(P(("parts", "fsdp", "dp"), None, None), P(("parts", "fsdp", "dp"), None)),
        check_vma=False,
    )
```

```python
import functools
import math

import jax
import jax.numpy as jnp
from jax import lax
from jax.experimental import pallas as pl
from jax.experimental.pallas import tpu as pltpu
from jax.sharding import PartitionSpec as P

TSTEP = 8
WIDE = 512
MESH = pl.DeviceIdType.MESH
BF16, F32 = jnp.bfloat16, jnp.float32


def cut(rows):
    return max(16, (rows * 5 + 128) // 16 // 16 * 16)


def kernel(
    n, heads,
    order_ref, counts_ref, gain_ref, tok_ref, shift_ref, wq_ref, wk_ref, wv_ref, wo_ref, cot_ref,
    mixed_ref, grad_ref,
    held, heldshift, shf, normed, buf, obuf, acc, att, cot, gmine, gsend, gsib, rrecv, rsend,
    mixs, gout,
    loc_sem, tok_sem, out_sem,
    a_ring, a_sib, a_x, a_sibx,
    b_ring, b_sib, b_x, b_sibx,
    gs_sem, r_sem,
):
    dp, fs, part = lax.axis_index("dp"), lax.axis_index("fsdp"), lax.axis_index("parts")
    rows = normed.shape[2]
    orows = wo_ref.shape[0]
    pa, pb = buf.shape[0] // 2, obuf.shape[0] // 2
    ma, mb = (n - 1) * pa, (n - 1) * pb
    tok_rows = normed.shape[1]
    slot = tok_rows // 2
    hd = att.shape[1] // heads
    rp = gmine.shape[2]
    gp = gmine.shape[1]
    rem, div = lax.rem, lax.div

    half = n // 2
    side = rem(fs, 2)
    r = (1 - side) * div(fs, 2) + side * (n - 1 - div(fs, 2))
    way = 1 - 2 * dp

    def at(q):
        q = rem(q + n, n)
        back = div(q, half)
        return (1 - back) * 2 * q + back * (2 * (n - 1 - q) + 1)

    nxt = {"fsdp": at(r + way)}
    prv = {"fsdp": at(r - way)}
    sib = {"dp": 1 - dp}
    xp = rem(part, 2)
    xdev = {"parts": part + 1 - 2 * xp}

    barrier = pltpu.get_barrier_semaphore()
    for dev in (nxt, prv, sib, xdev):
        pl.semaphore_signal(barrier, inc=1, device_id=dev, device_id_type=MESH)
    pl.semaphore_wait(barrier, 4)

    def rcopy(src, dst, sems, i, dev):
        return pltpu.make_async_remote_copy(
            src_ref=src, dst_ref=dst, send_sem=sems.at[0, i], recv_sem=sems.at[1, i],
            device_id=dev, device_id_type=MESH,
        )

    def part_rows(height):
        a = cut(height)
        ring = (a * xp, height - a)
        mine = ((height - a) * xp, a)
        other = ((height - a) * (1 - xp), a)
        return ring, mine, other

    def piece(ref, p, owner, height, span):
        start = pl.multiple_of(owner * height + span[0], 16)
        return ref.at[p, pl.ds(start, span[1]), :]

    ring_a, mine_a, other_a = part_rows(rows)
    ring_b, mine_b, other_b = part_rows(orows)

    class Gather:
        def __init__(self, ref, height, count, spans, ring, sibl, x, sibx):
            self.ref, self.height, self.count = ref, height, count
            self.ring_rows, self.mine, self.other = spans
            self.ring, self.sibl, self.x, self.sibx = ring, sibl, x, sibx
            self.total = (n - 1) * count

        def here(self, m):
            return at(r - way * (div(m, self.count) + 1)), dp * self.count + rem(m, self.count)

        def there(self, m):
            return at(r + way * (div(m, self.count) + 1)), (1 - dp) * self.count + rem(m, self.count)

        def cp(self, kind, m, where):
            owner, p = where
            span, sems, dev = {
                "ring": (self.ring_rows, self.ring, nxt),
                "sib": (self.ring_rows, self.sibl, sib),
                "x": (self.mine, self.x, xdev),
                "xin": (self.other, self.x, xdev),
                "sibx": (self.other, self.sibx, sib),
            }[kind]
            ref = piece(self.ref, p, owner, self.height, span)
            return rcopy(ref, ref, sems, m, dev)

        def step(self, m):
            w = self.here(m)
            self.cp("ring", m, w).wait_recv()

            @pl.when(m < self.total - self.count)
            def _():
                self.cp("ring", m + self.count, w).start()

            self.cp("x", m, w).start()
            self.cp("sib", m, w).start()

        def step_x(self, m):
            w = self.here(m)
            self.cp("xin", m, w).wait_recv()
            self.cp("sibx", m, w).start()

        def arrived(self, m):
            w = self.there(m)
            self.cp("sib", m, w).wait_recv()
            self.cp("sibx", m, w).wait_recv()

        def drain(self):
            @pl.loop(0, self.total)
            def _(m):
                w = self.here(m)
                self.cp("ring", m, w).wait_send()
                self.cp("x", m, w).wait_send()
                self.cp("sib", m, w).wait_send()
                self.cp("sibx", m, w).wait_send()

    ga = Gather(buf, rows, pa, (ring_a, mine_a, other_a), a_ring, a_sib, a_x, a_sibx)
    gb = Gather(obuf, orows, pb, (ring_b, mine_b, other_b), b_ring, b_sib, b_x, b_sibx)

    def own_cols(j):
        return pl.ds(pl.multiple_of((dp * pb + j) * WIDE, WIDE), WIDE)

    weights = (wq_ref, wk_ref, wv_ref)
    for j in range(pa):
        cols = pl.ds(pl.multiple_of(dp * WIDE, WIDE), WIDE)
        src = weights[j].at[pl.ds(pl.multiple_of(ring_a[0], 16), ring_a[1]), cols]
        dst = piece(buf, dp * pa + j, fs, rows, ring_a)
        rcopy(src, dst, a_ring, j, nxt).start()

    tok_in = held.at[pl.ds(dp * 2, 2)]
    tcopy = rcopy(tok_ref, tok_in, tok_sem, 0, sib)
    tcopy.start()
    scopy = rcopy(shift_ref, heldshift.at[dp], tok_sem, 1, sib)
    scopy.start()

    local = []

    def lcopy(src, dst):
        c = pltpu.make_async_copy(src, dst, loc_sem.at[len(local)])
        c.start()
        local.append(c)

    lcopy(tok_ref, tok_in)
    lcopy(shift_ref, heldshift.at[dp])
    for d in range(2):
        for j in range(pa):
            lcopy(
                weights[j].at[:, pl.ds(d * WIDE, WIDE)],
                piece(buf, d * pa + j, fs, rows, (0, rows)),
            )
    for p in range(2 * pb):
        lcopy(wo_ref.at[:, pl.ds(p * WIDE, WIDE)], piece(obuf, p, fs, orows, (0, orows)))
    lcopy(cot_ref, cot)

    def add(owner, p, first=False):
        start = pl.multiple_of(owner * rows, 16)
        term = jnp.dot(
            normed[owner], buf[p, pl.ds(start, rows), :], preferred_element_type=F32
        )
        if first:
            acc[p] = term
        else:
            acc[p] += term

    def add_here(m):
        add(*ga.here(m))

    def add_there(m):
        ga.arrived(m)
        add(*ga.there(m))

    lead, lag = 2 * pa, pa
    join = 3 * pa
    early = pb * (n - 4)

    def tick(b):
        @pl.when(b < mb)
        def _():
            gb.step(b)

        @pl.when((b >= lag) & (b < mb + lag))
        def _():
            gb.step_x(b - lag)


    @pl.loop(0, lead)
    def _(m):
        ga.step(m)

        @pl.when(m >= lag)
        def _():
            ga.step_x(m - lag)

    for c in local:
        c.wait()
    rcopy(tok_ref, held.at[pl.ds(2 - dp * 2, 2)], tok_sem, 0, sib).wait_recv()
    rcopy(shift_ref, heldshift.at[1 - dp], tok_sem, 1, sib).wait_recv()
    for d in range(2):
        shf[pl.ds(d * 16, 16), :] = heldshift[d].astype(F32)

    tile = 32
    per = slot // tile

    @pl.loop(0, 2 * per)
    def _(t):
        k = div(t, per)
        chosen = order_ref[0, dp * 2 + k]
        x = held[chosen, pl.ds(pl.multiple_of(rem(t, per) * tile, tile), tile), :].astype(F32)
        scale = lax.rsqrt(jnp.mean(x * x, axis=-1, keepdims=True) + 1e-05)
        y = (x * scale * gain_ref[...]).astype(BF16)
        at_rows = pl.ds(pl.multiple_of(t * tile, tile), tile)
        for c in range(n):
            normed[c, at_rows, :] = y[:, c * rows:(c + 1) * rows]

    @pl.loop(0, 2 * pa)
    def _(p):
        add(fs, p, True)

    @pl.loop(lead, ma + lag + 1)
    def _(m):
        @pl.when(m < ma)
        def _():
            ga.step(m)

        @pl.when(m == join - pa)
        def _():
            for j in range(pb):
                ref = piece(obuf, dp * pb + j, fs, orows, ring_b)
                rcopy(ref, ref, b_ring, j, nxt).start()

        over = m - join

        @pl.when((over >= 0) & (m < ma) & (rem(over, pa) < pb))
        def _():
            tick(div(over, pa) * pb + rem(over, pa))

        @pl.when(m < ma + lag)
        def _():
            ga.step_x(m - lag)
            add_here(m - lag)

        add_there(m - lag - 1)
        late = m - lead

        @pl.when(late < lead - lag)
        def _():
            add_here(late)

        @pl.when(late < lead - lag - 1)
        def _():
            add_there(late)

    per_half = heads // 2
    per_head = hd // (2 * rp)

    def attend(h, k):
        d = div(h, per_half)
        cols = pl.ds(pl.multiple_of(rem(h, per_half) * hd, hd), hd)
        rws = pl.ds(pl.multiple_of(k * slot, slot), slot)
        q = acc[d * 3, rws, cols].astype(BF16)
        kk = acc[d * 3 + 1, rws, cols].astype(BF16)
        v = acc[d * 3 + 2, rws, cols].astype(BF16)
        chosen = order_ref[0, dp * 2 + k]
        live = counts_ref[fs * 4 + chosen]
        row = shf[pl.ds(chosen * 8 + h, 1), :]
        s = lax.dot_general(q, kk, (((1,), (1,)), ((), ())), preferred_element_type=F32)
        s = s * (1.0 / math.sqrt(hd)) + row
        i = lax.broadcasted_iota(jnp.int32, (slot, slot), 0)
        j = lax.broadcasted_iota(jnp.int32, (slot, slot), 1)
        ok = ((j & (TSTEP - 1)) <= (i & (TSTEP - 1))) & (j < live * TSTEP)
        s = jnp.where(ok, s, -1e30)
        w = jnp.exp(s - jnp.max(s, axis=-1, keepdims=True))
        prob = (w * (1.0 / jnp.sum(w, axis=-1, keepdims=True))).astype(BF16)
        o = jnp.dot(prob, v, preferred_element_type=F32).astype(BF16)
        att[rws, pl.ds(pl.multiple_of(h * hd, hd), hd)] = o

    def gcopy(o):
        return rcopy(gsend.at[o], gsib.at[o], gs_sem, o, sib)

    def gradient(h):
        a = att[:, pl.ds(pl.multiple_of(h * hd, hd), hd)]
        for c in range(gp):
            g = lax.dot_general(
                a, cot[:, c * WIDE:(c + 1) * WIDE], (((0,), (0,)), ((), ())),
                preferred_element_type=F32,
            )
            for o in range(per_head):
                g0 = g[(2 * o) * rp:(2 * o + 1) * rp]
                g1 = g[(2 * o + 1) * rp:(2 * o + 2) * rp]
                gmine[h * per_head + o, c] = jnp.where(dp == 0, g0, g1)
                gsend[h * per_head + o, c] = jnp.where(dp == 0, g1, g0).astype(BF16)
        for o in range(per_head):
            gcopy(h * per_head + o).start()

    def mixcopy(k, c):
        cols = pl.ds(pl.multiple_of(c * WIDE, WIDE), WIDE)
        return pltpu.make_async_copy(
            mixs.at[k, :, cols], mixed_ref.at[k, :, cols], out_sem.at[k * 2 * pb + c]
        )

    def mix(t):
        k, c = rem(t, 2), div(t, 2)
        rws = pl.ds(pl.multiple_of(k * slot, slot), slot)
        cols = pl.ds(pl.multiple_of(c * WIDE, WIDE), WIDE)
        branch = jnp.dot(att[rws, :], obuf[c], preferred_element_type=F32)
        chosen = order_ref[0, dp * 2 + k]
        mixs[k, :, cols] = (held[chosen, :, cols].astype(F32) + branch).astype(BF16)
        mixcopy(k, c).start()

    def hop(m):
        return rcopy(rsend.at[m], rrecv.at[m], r_sem, m, nxt)

    scale = 1.0 / math.sqrt(tok_rows * n * 2)

    def reduce_step(m):
        s, c = div(m, gp), rem(m, gp)
        owner = at(r - way * (s + 1))

        @pl.when(c == 0)
        def _():
            gcopy(owner).wait_recv()

        @pl.when(s == 0)
        def _():
            rsend[m] = (gmine[owner, c] + gsib[owner, c].astype(F32)).astype(BF16)
            hop(m).start()

        @pl.when((s > 0) & (s < n - 1))
        def _():
            hop(m - gp).wait_recv()
            rsend[m] = (
                gmine[owner, c] + gsib[owner, c].astype(F32) + rrecv[m - gp].astype(F32)
            ).astype(BF16)
            hop(m).start()

        @pl.when(s == n - 1)
        def _():
            hop(m - gp).wait_recv()
            gout[:, pl.ds(pl.multiple_of(c * WIDE, WIDE), WIDE)] = scale * (
                gmine[owner, c] + gsib[owner, c].astype(F32) + rrecv[m - gp].astype(F32)
            )

    units = 2 * heads
    matched = n == heads
    ahead = 4
    begun = units - ahead if matched else 0

    def head_at(i):
        if not matched:
            return i
        return at(r + (2 * rem(i, 2) - 1) * (div(i, 2) + 1) - div(i, n - 1) * (n // 2))

    @pl.loop(0, max(mb - early + lag, units))
    def _(u):
        tick(early + u)

        if matched:
            @pl.when((u >= ahead) & (u < units))
            def _():
                reduce_step(u - ahead)

        @pl.when(u < units)
        def _():
            attend(head_at(div(u, 2)), rem(u, 2))

        @pl.when((u < units) & (rem(u, 2) == 1))
        def _():
            gradient(head_at(div(u, 2)))

    @pl.loop(0, mb)
    def _(m):
        gb.arrived(m)

    @pl.loop(begun, n * gp)
    def _(m):
        reduce_step(m)
        past = m - begun

        @pl.when((rem(past, 2) == 0) & (past < 8 * pb))
        def _():
            mix(div(past, 2))

    gcp = pltpu.make_async_copy(gout, grad_ref, out_sem.at[4 * pb])
    gcp.start()
    for k in range(2):
        for c in range(2 * pb):
            mixcopy(k, c).wait()

    ga.drain()
    gb.drain()
    tcopy.wait_send()
    scopy.wait_send()

    @pl.loop(0, n)
    def _(o):
        gcopy(o).wait_send()

    @pl.loop(0, (n - 1) * gp)
    def _(m):
        hop(m).wait_send()

    gcp.wait()


def body(n, tokens, key_shift, counts, repack_order, norm_gain, wq, wk, wv, wo, cotangent):
    scenes, slot, width = tokens.shape
    rows, proj = wq.shape
    orows = wo.shape[0]
    heads = key_shift.shape[1]
    tok_rows = scenes * slot
    rp = proj // (2 * n)
    gp = width // WIDE
    pa, pb = 3 * proj // 2 // WIDE, width // 2 // WIDE
    ma, mb = (n - 1) * pa, (n - 1) * pb
    dma = pltpu.SemaphoreType.DMA
    any_spec = pl.BlockSpec(memory_space=pl.ANY)
    smem = pl.BlockSpec(memory_space=pltpu.SMEM)
    vmem = pl.BlockSpec(memory_space=pltpu.VMEM)
    mixed, grad = pl.pallas_call(
        functools.partial(kernel, n, heads),
        out_shape=(
            jax.ShapeDtypeStruct((scenes, slot, width), BF16),
            jax.ShapeDtypeStruct((rp, width), F32),
        ),
        in_specs=[smem, smem, vmem] + [any_spec] * 7,
        out_specs=(any_spec, any_spec),
        scratch_shapes=[
            pltpu.VMEM((2 * scenes, slot, width), BF16),
            pltpu.VMEM((2, scenes * heads, slot), BF16),
            pltpu.VMEM((2 * scenes * heads, slot), F32),
            pltpu.VMEM((n, tok_rows, rows), BF16),
            pltpu.VMEM((2 * pa, n * rows, WIDE), BF16),
            pltpu.VMEM((2 * pb, n * orows, WIDE), BF16),
            pltpu.VMEM((2 * pa, tok_rows, WIDE), F32),
            pltpu.VMEM((tok_rows, proj), BF16),
            pltpu.VMEM((tok_rows, width), BF16),
            pltpu.VMEM((n, gp, rp, WIDE), F32),
            pltpu.VMEM((n, gp, rp, WIDE), BF16),
            pltpu.VMEM((n, gp, rp, WIDE), BF16),
            pltpu.VMEM(((n - 1) * gp, rp, WIDE), BF16),
            pltpu.VMEM(((n - 1) * gp, rp, WIDE), BF16),
            pltpu.VMEM((scenes, slot, width), BF16),
            pltpu.VMEM((rp, width), F32),
            dma((3 + 2 * pa + 2 * pb,)),
            dma((2, 2)),
            dma((4 * pb + 1,)),
            dma((2, ma)), dma((2, ma)), dma((2, ma)), dma((2, ma)),
            dma((2, mb)), dma((2, mb)), dma((2, mb)), dma((2, mb)),
            dma((2, n)),
            dma((2, (n - 1) * gp)),
        ],
        compiler_params=pltpu.CompilerParams(
            collective_id=0, has_side_effects=True, vmem_limit_bytes=60 * 1024 * 1024
        ),
    )(
        repack_order, counts, norm_gain.reshape(1, width), tokens,
        key_shift.reshape(scenes * heads, slot), wq, wk, wv, wo, cotangent.reshape(tok_rows, width),
    )
    return mixed, grad


def solution(mesh):
    return jax.shard_map(
        functools.partial(body, mesh.shape["fsdp"]),
        mesh=mesh,
        in_specs=(
            P(("parts", "fsdp", "dp"), None, None),
            P(("parts", "fsdp", "dp"), None, None),
            P("parts"),
            P(("parts", "fsdp"), None),
            P(),
            P("fsdp", None),
            P("fsdp", None),
            P("fsdp", None),
            P("fsdp", None),
            P(("parts", "fsdp", "dp"), None, None),
        ),
        out_specs=(P(("parts", "fsdp", "dp"), None, None), P(("parts", "fsdp", "dp"), None)),
        check_vma=False,
    )
```
